256 devices in a mesh: gx: 16 (over y, x), gy: 16 (over z, core).
Axes of the slice: x: 4, y: 4, z: 8, core: 2. Of those that a mesh axis runs over, the one named last changes fastest.
Arguments:
- field: float32 [768, 768, 256], P('gx', 'gy'), may hold values from -6 to 6
- stdev: float32 [768, 768, 256], P('gx', 'gy'), may hold values from 0.5 to 2
- mixing: float32 [4, 256, 256], replicated, may hold values from -0.375 to 0.375
- gen_weight: float32 [4, 256], replicated, may hold values from 0.5 to 4
Outputs:
- covariance_product: float32 [768, 768, 256], P('gx', 'gy')
The draws below stay inside these ranges and needn't reach their ends.
All inputs are finite; a program needn't handle non-finite values.
Results may differ from the reference program's by a relative error of at most 0.0001.
Values sent between devices are 32-bit elements; how exact they have to be, the bound alone decides.
A program may use at most 128 MiB of HBM per device.

```python
import math
import jax
import jax.numpy as jnp
from jax import lax

RAD = 3
GENS = 4
CH = 256
NX = 768
NY = 768


def block_scale(stream_key, dims, pieces, least, top_value):
    def one(dim, blocks):
        steps = jax.random.uniform(jax.random.fold_in(jax.random.fold_in(stream_key, 6), dim), (blocks,), jnp.float32, least / len(pieces), top_value / len(pieces))
        return jnp.repeat(jnp.exp(steps), dims[dim] // blocks).reshape((-1,) + (1,) * (len(dims) - dim - 1))

    gain = one(*pieces[0])
    for cut in pieces[1:]:
        gain = gain * one(*cut)
    return gain


def scatter_about(rng, shape, deviation, bound, pieces=(), held_as=jnp.bfloat16):
    entries = jax.random.normal(rng, shape, jnp.float32) * deviation
    if len(pieces) > 0:
        entries = block_scale(rng, shape, pieces, -0.22, 0.18) * entries
    return jnp.clip(entries, min=-bound, max=bound).astype(held_as)


def setup_inputs(seed: int = 0) -> dict:
    key_list = jax.random.split(jax.random.key(seed), 5)
    return {
        "field": scatter_about(key_list[0], (NX, NY, CH), 1.0, 6.0, ((0, 16), (1, 16)), jnp.float32),
        "stdev": jnp.clip(jnp.exp(math.log(2.0) - 1.3862944 * jax.random.uniform(key_list[1], (NX, NY, CH), jnp.float32) ** block_scale(key_list[1], (NX, NY, CH), ((0, 16), (1, 16)), -0.2, 0.2)), 0.5, 2.0),
        "mixing": scatter_about(key_list[2], (GENS, CH, CH), CH ** -0.5, 0.375, (), jnp.float32),
        "gen_weight": jnp.clip(jnp.exp(jax.random.uniform(key_list[3], (GENS, CH), jnp.float32, math.log(0.5), math.log(4.0))), 0.5, 4.0),
    }


def beta_weights():
    values = [(1.0 - (shift_k / (RAD + 1.0)) ** 2) ** 2 for shift_k in range(-RAD, RAD + 1)]
    total = sum(values)
    return [value / total for value in values]


def line_filter(values, axis_dim):
    weights = beta_weights()
    widths = [(0, 0), (0, 0), (0, 0)]
    widths[axis_dim] = (RAD, RAD)
    padded = jnp.pad(values, widths)
    length = values.shape[axis_dim]
    result = jnp.zeros_like(values)
    for offset, weight in enumerate(weights):
        result = result + weight * lax.slice_in_dim(padded, offset, offset + length, axis=axis_dim)
    return result


def smooth(values):
    return line_filter(line_filter(values, 0), 1)


def reference(field, stdev, mixing, gen_weight):
    upward = field * stdev
    levels = [upward]
    for generation in range(GENS - 1):
        smoothed = smooth(upward)
        rows, cols, chans = smoothed.shape
        upward = smoothed.reshape(rows // 2, 2, cols // 2, 2, chans).sum(axis=(1, 3)) * 0.5
        levels.append(upward)
    downward = None
    for generation in reversed(range(GENS)):
        current = levels[generation]
        rows, cols, chans = current.shape
        mixed = jnp.dot(current.reshape(rows * cols, chans), mixing[generation], precision=lax.Precision.HIGHEST)
        mixed = mixed.reshape(rows, cols, chans) * gen_weight[generation]
        if downward is not None:
            finer = jnp.repeat(jnp.repeat(downward, 2, axis=0), 2, axis=1) * 0.5
            mixed = mixed + finer
        downward = smooth(mixed)
    return stdev * downward
```

```python
import functools

import jax
import jax.numpy as jnp
from jax import lax
from jax.experimental import pallas as pl
from jax.experimental.pallas import tpu as pltpu
from jax.sharding import PartitionSpec as P

RAD = 3
GENS = 4
LANE = 128
MESH = pl.DeviceIdType.MESH
DIRS = [(1, 0), (-1, 0), (0, 1), (0, -1), (1, 1), (1, -1), (-1, 1), (-1, -1)]
N = (48, 24, 12, 6)
RIM = (3, 5, 6, 6)
OUT = (0, 2, 3, 3)
YO = 8

_total = sum((1.0 - (k / (RAD + 1.0)) ** 2) ** 2 for k in range(-RAD, RAD + 1))
B = [(1.0 - (k / (RAD + 1.0)) ** 2) ** 2 / _total for k in range(RAD + 1)]
DOWN = [B[3], B[2] + B[3], B[1] + B[2], B[0] + B[1], B[0] + B[1], B[1] + B[2], B[2] + B[3], B[3]]
EVEN = [B[3], B[1] + B[2], B[0] + B[1], B[2] + B[3]]
ODD = EVEN[::-1]


def loop(count, step, unroll=1):
    def one(i, carry):
        step(i)
        return carry

    lax.fori_loop(0, count, one, 0, unroll=unroll)


def filtered(load):
    return load(3) * B[0] + (load(2) + load(4)) * B[1] + (load(1) + load(5)) * B[2] + (load(0) + load(6)) * B[3]


def restricted(load):
    return (
        (load(3) + load(4)) * DOWN[3]
        + (load(2) + load(5)) * DOWN[2]
        + (load(1) + load(6)) * DOWN[1]
        + (load(0) + load(7)) * DOWN[0]
    )


def dotted(weights, parts, scale=1.0):
    total = parts[0] * (weights[0] * scale)
    for weight, part in zip(weights[1:], parts[1:]):
        total = total + part * (weight * scale)
    return total


def restrict_rows(src, first, count, cols, dst, rows, shift, dst_cols):
    whole = [i for i in range(rows) if 2 * i - shift >= 0 and 2 * i - shift + 7 < count]
    low, high = whole[0], whole[-1] + 1
    for half in range(2):
        for i in list(range(low)) + list(range(high, rows)):
            taps = [t for t in range(8) if 0 <= 2 * i - shift + t < count]
            parts = [src[first + 2 * i - shift + t, half, cols] for t in taps]
            dst[i, half, dst_cols] = dotted([DOWN[t] for t in taps], parts, 0.5)

    def step(j):
        for half in range(2):
            base = first + 2 * (j + low) - shift
            dst[j + low, half, dst_cols] = restricted(lambda t: src[base + t, half, cols]) * 0.5

    loop(high - low, step, 2)


def restrict_cols(src, start, dst, rows, cols):
    def step(i):
        for half in range(2):
            dst[i, half] = restricted(lambda t: src[i, half, pl.ds(start + t, cols, stride=2)])

    loop(rows, step, 2)


def filter_cols(src, start, dst, rows, cols):
    def step(i):
        for half in range(2):
            dst[i, half] = filtered(lambda t: src[i, half, pl.ds(start + t, cols)])

    loop(rows, step, 2)


def filter_rows(src, dst, rows):
    def step(i):
        for half in range(2):
            dst[i, half] = filtered(lambda t: src[i + t, half])

    loop(rows, step, 2)


def prolong_cols(src, dst, rows, count, odd_first):
    def step(i):
        for half in range(2):
            parts = [src[i, half, pl.ds(t, count)] for t in range(4 if odd_first else 5)]
            if odd_first:
                lead, next_one = dotted(ODD, parts), dotted(EVEN, parts)
            else:
                lead, next_one = dotted(EVEN, parts[:4]), dotted(ODD, parts[1:])
            dst[i, half, pl.ds(0, count, stride=2)] = lead
            dst[i, half, pl.ds(1, count, stride=2)] = next_one

    loop(rows, step, 2)


def prolong_rows(src, m, half, odd_first):
    parts = [src[m + t, half] for t in range(4 if odd_first else 5)]
    if odd_first:
        return dotted(ODD, parts, 0.5), dotted(EVEN, parts, 0.5)
    return dotted(EVEN, parts[:4], 0.5), dotted(ODD, parts[1:], 0.5)


def mix(ref, weights, gen, rows_each, steps, cols, unroll):
    count = rows_each * cols

    def step(i):
        rows = pl.ds(i * rows_each, rows_each)
        cells = jnp.concatenate([ref[rows, half].reshape(count, LANE) for half in range(2)], axis=1)
        high = cells.astype(jnp.bfloat16)
        low = (cells - high.astype(jnp.float32)).astype(jnp.bfloat16)
        product = jnp.dot(
            jnp.concatenate([high, high, low], axis=1), weights[gen], preferred_element_type=jnp.float32
        )
        for half in range(2):
            ref[rows, half] = product[:, half * LANE : (half + 1) * LANE].reshape(rows_each, cols, LANE)

    loop(steps, step, unroll)


def kernel(
    size_x, size_y, field, stdev, mixing, gen_weight, out,
    u0, u1, u2, u3, sd, mats, gains, weights,
    x1, x2, x3, c1, c2, c3,
    rx1, rx2, rx3, ry1, ry2, ry3, rc1, rc2, rc3,
    y0, y1, y2, y3, d0, d1, d2, d3, t1, t2, t3,
    load_sem, send_sem, recv_sem,
):
    gx, gy = lax.axis_index("gx"), lax.axis_index("gy")
    ext = (u0, u1, u2, u3)
    west, east = gx == 0, gx == size_x - 1
    south, north = gy == 0, gy == size_y - 1

    def there(d):
        nx, ny = gx + d[0], gy + d[1]
        return (nx >= 0) & (nx < size_x) & (ny >= 0) & (ny < size_y)

    def against(d):
        return (-d[0], -d[1])

    loads = []
    for part, (row, count) in enumerate(((0, 8), (40, 8), (8, 32))):
        for half in range(2):
            lanes = pl.ds(half * LANE, LANE)
            rows = pl.ds(row, count)
            loads.append(
                pltpu.make_async_copy(
                    field.at[rows, :, lanes], u0.at[pl.ds(row + RAD, count), half, pl.ds(YO, N[0])],
                    load_sem.at[part * 4 + half * 2],
                )
            )
            loads.append(
                pltpu.make_async_copy(
                    stdev.at[rows, :, lanes], sd.at[rows, half], load_sem.at[part * 4 + half * 2 + 1]
                )
            )
    loads.append(pltpu.make_async_copy(mixing, mats, load_sem.at[12]))
    loads.append(pltpu.make_async_copy(gen_weight, gains, load_sem.at[13]))
    for copy in loads:
        copy.start()

    barrier = pltpu.get_barrier_semaphore()
    for d in DIRS:

        @pl.when(there(d))
        def _():
            pl.semaphore_signal(barrier, inc=1, device_id=(gx + d[0], gy + d[1]), device_id_type=MESH)

    def gather_copy(gen, k):
        d, n, rim, buf = DIRS[k], N[gen], RIM[gen], ext[gen]

        def ranges(step, first):
            if step == 0:
                return pl.ds(first, n), pl.ds(first, n)
            if step > 0:
                return pl.ds(first + n - rim, rim), pl.ds(first - rim, rim)
            return pl.ds(first, rim), pl.ds(first + n, rim)

        (sx, tx), (sy, ty) = ranges(d[0], rim), ranges(d[1], YO)
        slot = gen * 8 + k
        return pltpu.make_async_remote_copy(
            src_ref=buf.at[sx, :, sy], dst_ref=buf.at[tx, :, ty],
            send_sem=send_sem.at[slot], recv_sem=recv_sem.at[slot],
            device_id=(gx + d[0], gy + d[1]), device_id_type=MESH,
        )

    def landing(gen, k):
        rx, ry, rc = ((rx1, ry1, rc1), (rx2, ry2, rc2), (rx3, ry3, rc3))[gen - 1]
        n, e = N[gen], OUT[gen]
        if k < 2:
            return rx.at[k, :, :, pl.ds(0, n)]
        if k < 4:
            return ry.at[k - 2, :, :, pl.ds(0, e)]
        return rc.at[k - 4, :, :, pl.ds(0, e)]

    def scatter_copy(gen, k):
        d, n, e, buf = DIRS[k], N[gen], OUT[gen], (c1, c2, c3)[gen - 1]

        def span(step):
            return pl.ds(e, n) if step == 0 else pl.ds(n + e, e) if step > 0 else pl.ds(0, e)

        slot = (gen + 3) * 8 + k
        return pltpu.make_async_remote_copy(
            src_ref=buf.at[span(d[0]), :, span(d[1])], dst_ref=landing(gen, k),
            send_sem=send_sem.at[slot], recv_sem=recv_sem.at[slot],
            device_id=(gx + d[0], gy + d[1]), device_id_type=MESH,
        )

    def start(make, gen, ks=range(8)):
        for k in ks:
            pl.when(there(DIRS[k]))(lambda k=k: make(gen, k).start())

    def arrive(make, gen):
        for k in range(8):
            pl.when(there(against(DIRS[k])))(lambda k=k: make(gen, k).wait_recv())

    def sent(make, gen):
        for k in range(8):
            pl.when(there(DIRS[k]))(lambda k=k: make(gen, k).wait_send())

    def clear(buf, rows, cols):
        loop(rows, lambda i: buf.__setitem__((i, slice(None), cols), jnp.zeros((2, cols.stop - cols.start, LANE), jnp.float32)))

    clear(x1, 28, slice(0, 8))
    clear(x1, 28, slice(56, 72))
    clear(x2, 18, slice(0, 8))
    clear(x2, 18, slice(40, 56))
    clear(x3, 12, slice(0, 8))
    clear(x3, 12, slice(32, 40))

    def clear_edges(buf, width, n, first_y, rows, whole_rows):
        cols = buf.shape[2]
        last = width + n

        def rows_at(first):
            for i in range(width):
                buf[first + i] = jnp.zeros((2, cols, LANE), jnp.float32)

        pl.when(west)(lambda: rows_at(0))
        pl.when(east)(lambda: rows_at(last))
        pl.when(south)(lambda: clear(buf, rows, slice(first_y - width, first_y)))
        pl.when(north)(lambda: clear(buf, rows, slice(first_y + n, first_y + n + width)))

    for gen in range(GENS):
        clear_edges(ext[gen], RIM[gen], N[gen], YO, N[gen] + 2 * RIM[gen], True)
    for gen in range(1, GENS):
        rx, ry, rc = ((rx1, ry1, rc1), (rx2, ry2, rc2), (rx3, ry3, rc3))[gen - 1]
        for k in range(8):
            buf, at = ((rx, k) if k < 2 else (ry, k - 2) if k < 4 else (rc, k - 4))

            @pl.when(jnp.logical_not(there(against(DIRS[k]))))
            def _():
                buf[at] = jnp.zeros(buf.shape[1:], jnp.float32)

    def scale_rows(row, count):
        def step(i):
            for half in range(2):
                u0[RAD + row + i, half, YO : YO + N[0]] = u0[RAD + row + i, half, YO : YO + N[0]] * sd[row + i, half]

        loop(count, step, 2)

    for copy in loads[:8]:
        copy.wait()
    scale_rows(0, 8)
    scale_rows(40, 8)
    near_x = 3 - west.astype(jnp.int32) - east.astype(jnp.int32)
    near_y = 3 - south.astype(jnp.int32) - north.astype(jnp.int32)
    pl.semaphore_wait(barrier, near_x * near_y - 1)
    start(gather_copy, 0, (0, 1, 4, 5, 6, 7))
    for copy in loads[8:12]:
        copy.wait()
    scale_rows(8, 32)
    start(gather_copy, 0, (2, 3))

    block = slice(YO, YO + N[0])
    restrict_rows(u0, RAD, N[0], block, x1, 28, 7, block)
    restrict_cols(x1, 1, c1, 28, 32)
    clear_edges(c1, 2, 24, 2, 28, True)
    start(scatter_copy, 1)
    restrict_rows(c1, 0, 28, slice(0, 32), x2, 18, 7, slice(8, 40))
    restrict_cols(x2, 1, c2, 18, 24)
    clear_edges(c2, 3, 12, 3, 18, True)
    start(scatter_copy, 2)
    restrict_rows(c2, 0, 18, slice(0, 24), x3, 12, 6, slice(8, 32))
    restrict_cols(x3, 2, c3, 12, 16)
    start(scatter_copy, 3)

    loads[12].wait()
    loads[13].wait()
    for gen in range(GENS):

        def split(i, gen=gen):
            rows = pl.ds(pl.multiple_of(i * 64, 64), 64)
            scaled = mats[gen, rows, :] * gains[gen : gen + 1, :]
            high = scaled.astype(jnp.bfloat16)
            low = (scaled - high.astype(jnp.float32)).astype(jnp.bfloat16)
            weights[gen, pl.ds(pl.multiple_of(i * 64, 64), 64), :] = high
            weights[gen, pl.ds(pl.multiple_of(i * 64 + 256, 64), 64), :] = low
            weights[gen, pl.ds(pl.multiple_of(i * 64 + 512, 64), 64), :] = high

        loop(4, split)
    arrive(gather_copy, 0)
    filter_cols(u0, YO - RAD, y0, 54, N[0])
    filter_rows(y0, d0, N[0])

    def add_up(gen):
        n, e, rim, buf, own = N[gen], OUT[gen], RIM[gen], ext[gen], (c1, c2, c3)[gen - 1]
        rx, ry, rc = ((rx1, ry1, rc1), (rx2, ry2, rc2), (rx3, ry3, rc3))[gen - 1]
        low, high = slice(YO, YO + e), slice(YO + n - e, YO + n)
        inner = slice(YO, YO + n)

        def step(i):
            for half in range(2):
                buf[rim + i, half, inner] = own[e + i, half, e : e + n]
                buf[rim + i, half, low] = buf[rim + i, half, low] + ry[0, i, half, 0:e]
                buf[rim + i, half, high] = buf[rim + i, half, high] + ry[1, i, half, 0:e]

        loop(n, step, 2)
        for i in range(e):
            for half in range(2):
                for side, row in ((0, rim + i), (1, rim + n - e + i)):
                    buf[row, half, inner] = buf[row, half, inner] + rx[side, i, half, 0:n]
                    buf[row, half, low] = buf[row, half, low] + rc[2 * side, i, half, 0:e]
                    buf[row, half, high] = buf[row, half, high] + rc[2 * side + 1, i, half, 0:e]

    for gen in (3, 2, 1):
        arrive(scatter_copy, gen)
        add_up(gen)
        start(gather_copy, gen)

    mix(d0, weights, 0, 4, 12, N[0], 2)

    arrive(gather_copy, 3)
    filter_cols(u3, YO - 6, y3, 18, 16)
    filter_rows(y3, d3, 12)
    mix(d3, weights, 3, 12, 1, 16, 1)
    clear_edges(d3, 3, 6, 3, 12, True)
    prolong_cols(d3, t3, 12, 12, True)
    arrive(gather_copy, 2)
    filter_cols(u2, YO - 6, y2, 24, 24)
    filter_rows(y2, d2, 18)
    mix(d2, weights, 2, 9, 2, 24, 1)

    def add_2(m):
        for half in range(2):
            first, second = prolong_rows(t3, m, half, True)
            d2[2 * m, half] = d2[2 * m, half] + first
            d2[2 * m + 1, half] = d2[2 * m + 1, half] + second

    loop(9, add_2)
    clear_edges(d2, 3, 12, 3, 18, True)
    prolong_cols(d2, t2, 18, 16, False)
    arrive(gather_copy, 1)
    filter_cols(u1, YO - 5, y1, 34, 32)
    filter_rows(y1, d1, 28)
    mix(d1, weights, 1, 4, 7, 32, 1)

    def add_1(m):
        for half in range(2):
            first, second = prolong_rows(t2, m, half, False)
            d1[2 * m, half] = d1[2 * m, half] + first
            d1[2 * m + 1, half] = d1[2 * m + 1, half] + second

    loop(14, add_1)
    clear_edges(d1, 2, 24, 2, 28, True)
    prolong_cols(d1, t1, 28, 24, False)

    def finish(m):
        for half in range(2):
            lanes = slice(half * LANE, (half + 1) * LANE)
            first, second = prolong_rows(t1, m, half, False)
            out[2 * m, :, lanes] = (d0[2 * m, half] + first) * sd[2 * m, half]
            out[2 * m + 1, :, lanes] = (d0[2 * m + 1, half] + second) * sd[2 * m + 1, half]

    loop(24, finish, 2)
    for gen in range(GENS):
        sent(gather_copy, gen)
    for gen in range(1, GENS):
        sent(scatter_copy, gen)


def solution(mesh):
    size_x, size_y = mesh.shape["gx"], mesh.shape["gy"]

    def body(field, stdev, mixing, gen_weight):
        def vmem(*shape, dtype=jnp.float32):
            return pltpu.VMEM(shape, dtype)

        def planes(x, y):
            return vmem(x, 2, y, LANE)

        return pl.pallas_call(
            functools.partial(kernel, size_x, size_y),
            out_shape=jax.ShapeDtypeStruct(field.shape, jnp.float32),
            in_specs=[pl.BlockSpec(memory_space=pltpu.HBM)] * 4,
            out_specs=pl.BlockSpec(memory_space=pltpu.VMEM),
            scratch_shapes=[
                planes(54, 64), planes(34, 48), planes(24, 32), planes(18, 24),
                planes(48, 48), vmem(4, 256, 256), vmem(4, 256), vmem(4, 768, 256, dtype=jnp.bfloat16),
                planes(28, 72), planes(18, 56), planes(12, 40),
                planes(28, 32), planes(18, 24), planes(12, 16),
                vmem(2, 2, 2, 24, LANE), vmem(2, 3, 2, 16, LANE), vmem(2, 3, 2, 8, LANE),
                vmem(2, 24, 2, 8, LANE), vmem(2, 12, 2, 8, LANE), vmem(2, 6, 2, 8, LANE),
                vmem(4, 2, 2, 8, LANE), vmem(4, 3, 2, 8, LANE), vmem(4, 3, 2, 8, LANE),
                planes(54, 48), planes(34, 32), planes(24, 24), planes(18, 16),
                planes(48, 48), planes(28, 32), planes(18, 24), planes(12, 16),
                planes(28, 48), planes(18, 32), planes(12, 24),
                pltpu.SemaphoreType.DMA((14,)),
                pltpu.SemaphoreType.DMA((56,)),
                pltpu.SemaphoreType.DMA((56,)),
            ],
            compiler_params=pltpu.CompilerParams(
                collective_id=0, has_side_effects=True, vmem_limit_bytes=44 * 2**20
            ),
            cost_estimate=pl.CostEstimate(flops=2 * 3556 * 768 * 256, bytes_accessed=8 * 2**20, transcendentals=0),
            name="multigrid",
        )(field, stdev, mixing, gen_weight)

    return jax.shard_map(
        body,
        mesh=mesh,
        in_specs=(P("gx", "gy", None), P("gx", "gy", None), P(), P()),
        out_specs=P("gx", "gy", None),
        check_vma=False,
    )
```

```python
import functools

import jax
import jax.numpy as jnp
from jax import lax
from jax.experimental import pallas as pl
from jax.experimental.pallas import tpu as pltpu
from jax.sharding import PartitionSpec as P

RAD = 3
GENS = 4
LANE = 128
MESH = pl.DeviceIdType.MESH
DIRS = [(1, 0), (-1, 0), (0, 1), (0, -1), (1, 1), (1, -1), (-1, 1), (-1, -1)]
N = (48, 24, 12, 6)
RIM = (3, 5, 6, 6)
OUT = (0, 2, 3, 3)
YO = 8

_total = sum((1.0 - (k / (RAD + 1.0)) ** 2) ** 2 for k in range(-RAD, RAD + 1))
B = [(1.0 - (k / (RAD + 1.0)) ** 2) ** 2 / _total for k in range(RAD + 1)]
DOWN = [B[3], B[2] + B[3], B[1] + B[2], B[0] + B[1], B[0] + B[1], B[1] + B[2], B[2] + B[3], B[3]]
EVEN = [B[3], B[1] + B[2], B[0] + B[1], B[2] + B[3]]
ODD = EVEN[::-1]


def loop(count, step, unroll=1):
    def one(i, carry):
        step(i)
        return carry

    lax.fori_loop(0, count, one, 0, unroll=unroll)


def filtered(load):
    return load(3) * B[0] + (load(2) + load(4)) * B[1] + (load(1) + load(5)) * B[2] + (load(0) + load(6)) * B[3]


def restricted(load):
    return (
        (load(3) + load(4)) * DOWN[3]
        + (load(2) + load(5)) * DOWN[2]
        + (load(1) + load(6)) * DOWN[1]
        + (load(0) + load(7)) * DOWN[0]
    )


def dotted(weights, parts, scale=1.0):
    total = parts[0] * (weights[0] * scale)
    for weight, part in zip(weights[1:], parts[1:]):
        total = total + part * (weight * scale)
    return total


def restrict_rows(src, first, count, dst, span, shift, cols, dst_first):
    whole = [i for i in span if 2 * i - shift >= 0 and 2 * i - shift + 7 < count]
    low, high = whole[0], whole[-1] + 1
    dst_cols = slice(dst_first, dst_first + cols)
    for half in range(2):
        for i in [i for i in span if i not in whole]:
            taps = [t for t in range(8) if 0 <= 2 * i - shift + t < count]
            parts = [src[first + 2 * i - shift + t, half, 0:cols] for t in taps]
            dst[i, half, dst_cols] = dotted([DOWN[t] for t in taps], parts, 0.5)

    def step(j):
        for half in range(2):
            base = first + 2 * (j + low) - shift
            dst[j + low, half, dst_cols] = restricted(lambda t: src[base + t, half, 0:cols]) * 0.5

    loop(high - low, step, 4)


def restrict_cols(src, start, dst, rows, cols):
    def step(i):
        for half in range(2):
            dst[i, half] = restricted(lambda t: src[i, half, pl.ds(start + t, cols, stride=2)])

    loop(rows, step, 2)


def filter_cols(src, start, dst, rows, cols):
    def step(i):
        for half in range(2):
            dst[i, half] = filtered(lambda t: src[i, half, pl.ds(start + t, cols)])

    loop(rows, step, 2)


def filter_rows(src, dst, rows, cols):
    def step(i):
        for half in range(2):
            dst[i, half, YO : YO + cols] = filtered(lambda t: src[i + t, half, 0:cols])

    loop(rows, step, 2)


def prolong_cols(src, dst, rows, count, odd_first):
    def step(i):
        for half in range(2):
            parts = [src[i, half, pl.ds(t, count)] for t in range(4 if odd_first else 5)]
            if odd_first:
                lead, next_one = dotted(ODD, parts), dotted(EVEN, parts)
            else:
                lead, next_one = dotted(EVEN, parts[:4]), dotted(ODD, parts[1:])
            dst[i, half, pl.ds(0, count, stride=2)] = lead
            dst[i, half, pl.ds(1, count, stride=2)] = next_one

    loop(rows, step, 2)


def prolong_rows(src, m, half, odd_first):
    parts = [src[m + t, half] for t in range(4 if odd_first else 5)]
    if odd_first:
        return dotted(ODD, parts, 0.5), dotted(EVEN, parts, 0.5)
    return dotted(EVEN, parts[:4], 0.5), dotted(ODD, parts[1:], 0.5)


def mix(src, dst, weights, gen, first, rows_each, steps, cols):
    count = rows_each * cols

    def step(i):
        rows = pl.ds(first + i * rows_each, rows_each)
        cells = jnp.concatenate([src[rows, half].reshape(count, LANE) for half in range(2)], axis=1)
        high = cells.astype(jnp.bfloat16)
        low = (cells - high.astype(jnp.float32)).astype(jnp.bfloat16)
        product = jnp.dot(
            jnp.concatenate([high, high, low], axis=1), weights[gen], preferred_element_type=jnp.float32
        )
        for half in range(2):
            dst[rows, half] = product[:, half * LANE : (half + 1) * LANE].reshape(rows_each, cols, LANE)

    loop(steps, step)


def kernel(
    size_x, size_y, field, stdev, mixing, gen_weight, out,
    u0, u1, u2, u3, sd, mats, gains, weights,
    x1, x2, x3, c1, c2, c3,
    rx1, rx2, rx3, ry1, ry2, ry3, rc1, rc2, rc3,
    w0, w1, w2, w3, k0, k1, k2, k3, d0, d1, d2, d3, t1, t2, t3,
    load_sem, send_sem, recv_sem,
):
    gx, gy = lax.axis_index("gx"), lax.axis_index("gy")
    west, east = gx == 0, gx == size_x - 1
    south, north = gy == 0, gy == size_y - 1
    wide, tall = (u0, u1, u2, u3), (w0, w1, w2, w3)
    landings = ((rx1, ry1, rc1), (rx2, ry2, rc2), (rx3, ry3, rc3))

    def there(d):
        nx, ny = gx + d[0], gy + d[1]
        return (nx >= 0) & (nx < size_x) & (ny >= 0) & (ny < size_y)

    def against(d):
        return (-d[0], -d[1])

    loads = []
    for row, count in ((0, 8), (40, 8), (8, 16), (24, 16)):
        for half in range(2):
            lanes, rows = pl.ds(half * LANE, LANE), pl.ds(row, count)
            for src, dst in ((field, u0.at[pl.ds(row + RAD, count), half]), (stdev, sd.at[rows, half])):
                loads.append(pltpu.make_async_copy(src.at[rows, :, lanes], dst, load_sem.at[len(loads)]))
    for src, dst in ((mixing, mats), (gen_weight, gains)):
        loads.append(pltpu.make_async_copy(src, dst, load_sem.at[len(loads)]))
    for copy in loads:
        copy.start()

    barrier = pltpu.get_barrier_semaphore()
    for d in DIRS:

        @pl.when(there(d))
        def _():
            pl.semaphore_signal(barrier, inc=1, device_id=(gx + d[0], gy + d[1]), device_id_type=MESH)

    def remote(src, dst, slot, d):
        return pltpu.make_async_remote_copy(
            src_ref=src, dst_ref=dst, send_sem=send_sem.at[slot], recv_sem=recv_sem.at[slot],
            device_id=(gx + d[0], gy + d[1]), device_id_type=MESH,
        )

    def rim_span(step, first, n, rim):
        if step > 0:
            return pl.ds(first + n - rim, rim), pl.ds(first - rim, rim)
        return pl.ds(first, rim), pl.ds(first + n, rim)

    def gather_x(gen, k):
        n, rim, buf = N[gen], RIM[gen], wide[gen]
        src, dst = rim_span(DIRS[k][0], rim, n, rim)
        return remote(buf.at[src, :, pl.ds(0, n)], buf.at[dst, :, pl.ds(0, n)], gen * 2 + k, DIRS[k])

    def gather_y(gen, k):
        n, rim, buf = N[gen], RIM[gen], tall[gen]
        src, dst = rim_span(DIRS[k][1], YO, n, rim)
        return remote(buf.at[:, :, src], buf.at[:, :, dst], 8 + gen * 2 + k - 2, DIRS[k])

    def scatter(gen, k):
        d, n, e, buf = DIRS[k], N[gen], OUT[gen], (c1, c2, c3)[gen - 1]
        rx, ry, rc = landings[gen - 1]
        if k < 2:
            dst = rx.at[k, :, :, pl.ds(0, n)]
        elif k < 4:
            dst = ry.at[k - 2, :, :, pl.ds(0, e)]
        else:
            dst = rc.at[k - 4, :, :, pl.ds(0, e)]

        def span(step):
            return pl.ds(e, n) if step == 0 else pl.ds(n + e, e) if step > 0 else pl.ds(0, e)

        return remote(buf.at[span(d[0]), :, span(d[1])], dst, 16 + (gen - 1) * 8 + k, d)

    ways = {gather_x: (0, 1), gather_y: (2, 3), scatter: (4, 5, 6, 7, 0, 1, 2, 3)}
    open_sends, open_receives = [], []

    def start(make, gen):
        open_sends.append((make, gen))
        open_receives.append((make, gen))
        for k in ways[make]:
            pl.when(there(DIRS[k]))(lambda k=k: make(gen, k).start())

    def arrive(make, gen):
        open_receives.remove((make, gen))
        for k in ways[make]:
            pl.when(there(against(DIRS[k])))(lambda k=k: make(gen, k).wait_recv())

    def sent(make, gen):
        for k in ways[make]:
            pl.when(there(DIRS[k]))(lambda k=k: make(gen, k).wait_send())

    def clear_cols(buf, rows, first, count):
        def step(i):
            buf[i, :, first : first + count] = jnp.zeros((2, count, LANE), jnp.float32)

        loop(rows, step, 2)

    def clear_rows(buf, first, count):
        for i in range(count):
            buf[first + i] = jnp.zeros(buf.shape[1:], jnp.float32)

    def clear_edges(buf, width, n):
        pl.when(west)(lambda: clear_rows(buf, 0, width))
        pl.when(east)(lambda: clear_rows(buf, width + n, width))
        pl.when(south)(lambda: clear_cols(buf, n + 2 * width, 0, width))
        pl.when(north)(lambda: clear_cols(buf, n + 2 * width, width + n, width))

    clear_cols(x1, 28, 0, 8)
    clear_cols(x1, 28, 56, 16)
    clear_cols(x2, 18, 0, 8)
    clear_cols(x2, 18, 40, 16)
    clear_cols(x3, 12, 0, 8)
    clear_cols(x3, 12, 32, 8)
    for gen in range(GENS):
        n, rim, rows = N[gen], RIM[gen], N[gen] + 2 * OUT[gen]
        pl.when(west)(lambda: clear_rows(wide[gen], 0, rim))
        pl.when(east)(lambda: clear_rows(wide[gen], rim + n, rim))
        pl.when(south)(lambda: clear_cols(tall[gen], rows, YO - rim, rim))
        pl.when(north)(lambda: clear_cols(tall[gen], rows, YO + n, rim))
    for gen in range(1, GENS):
        rx, ry, rc = landings[gen - 1]
        for k in range(8):
            buf, at = (rx, k) if k < 2 else (ry, k - 2) if k < 4 else (rc, k - 4)

            @pl.when(jnp.logical_not(there(against(DIRS[k]))))
            def _():
                buf[at] = jnp.zeros(buf.shape[1:], jnp.float32)

    def scale_rows(row, count):
        def step(i):
            for half in range(2):
                u0[RAD + row + i, half] = u0[RAD + row + i, half] * sd[row + i, half]

        loop(count, step, 2)

    for copy in loads[:8]:
        copy.wait()
    scale_rows(0, 8)
    scale_rows(40, 8)
    near_x = 3 - west.astype(jnp.int32) - east.astype(jnp.int32)
    near_y = 3 - south.astype(jnp.int32) - north.astype(jnp.int32)
    pl.semaphore_wait(barrier, near_x * near_y - 1)
    start(gather_x, 0)
    for copy in loads[8:12]:
        copy.wait()
    scale_rows(8, 16)
    restrict_rows(u0, RAD, N[0], x1, range(0, 12), 7, N[0], YO)
    for copy in loads[12:16]:
        copy.wait()
    scale_rows(24, 16)
    restrict_rows(u0, RAD, N[0], x1, range(12, 28), 7, N[0], YO)
    restrict_cols(x1, 1, c1, 28, 32)
    clear_edges(c1, 2, 24)
    start(scatter, 1)
    restrict_rows(c1, 0, 28, x2, range(18), 7, 32, 8)
    restrict_cols(x2, 1, c2, 18, 24)
    clear_edges(c2, 3, 12)
    start(scatter, 2)
    restrict_rows(c2, 0, 18, x3, range(12), 6, 24, 8)
    restrict_cols(x3, 2, c3, 12, 16)
    start(scatter, 3)
    for copy in loads[16:]:
        copy.wait()
    for gen in range(GENS):

        def split(i, gen=gen):
            scaled = mats[gen, pl.ds(pl.multiple_of(i * 64, 64), 64), :] * gains[gen : gen + 1, :]
            high = scaled.astype(jnp.bfloat16)
            low = (scaled - high.astype(jnp.float32)).astype(jnp.bfloat16)
            for place, part in ((0, high), (256, low), (512, high)):
                weights[gen, pl.ds(pl.multiple_of(i * 64 + place, 64), 64), :] = part

        loop(4, split)
    arrive(gather_x, 0)
    filter_rows(u0, w0, N[0], N[0])
    start(gather_y, 0)
    def add_up(gen):
        n, e, rim, buf, own = N[gen], OUT[gen], RIM[gen], wide[gen], (c1, c2, c3)[gen - 1]
        rx, ry, rc = landings[gen - 1]
        low, high = slice(0, e), slice(n - e, n)

        def step(i):
            for half in range(2):
                buf[rim + i, half, 0:n] = own[e + i, half, e : e + n]
                buf[rim + i, half, low] = buf[rim + i, half, low] + ry[0, i, half, 0:e]
                buf[rim + i, half, high] = buf[rim + i, half, high] + ry[1, i, half, 0:e]

        loop(n, step, 2)
        for i in range(e):
            for half in range(2):
                for side, row in ((0, rim + i), (1, rim + n - e + i)):
                    buf[row, half, 0:n] = buf[row, half, 0:n] + rx[side, i, half, 0:n]
                    buf[row, half, low] = buf[row, half, low] + rc[2 * side, i, half, 0:e]
                    buf[row, half, high] = buf[row, half, high] + rc[2 * side + 1, i, half, 0:e]

    for gen in (1, 2, 3):
        arrive(scatter, gen)
        add_up(gen)
        start(gather_x, gen)
    arrive(gather_y, 0)
    filter_cols(w0, YO - RAD, k0, N[0], N[0])
    mix(k0, d0, weights, 0, 0, 8, 3, N[0])
    for gen in (1, 2, 3):
        arrive(gather_x, gen)
        filter_rows(wide[gen], tall[gen], N[gen] + 2 * OUT[gen], N[gen])
        start(gather_y, gen)
    mix(k0, d0, weights, 0, 24, 8, 3, N[0])
    arrive(gather_y, 1)
    filter_cols(w1, YO - 5, k1, 28, 32)
    mix(k1, d1, weights, 1, 0, 14, 2, 32)
    arrive(gather_y, 2)
    filter_cols(w2, YO - 6, k2, 18, 24)
    mix(k2, d2, weights, 2, 0, 18, 1, 24)
    arrive(gather_y, 3)
    filter_cols(w3, YO - 6, k3, 12, 16)
    mix(k3, d3, weights, 3, 0, 12, 1, 16)
    clear_edges(d3, 3, 6)
    prolong_cols(d3, t3, 12, 12, True)

    def add_2(m):
        for half in range(2):
            first, second = prolong_rows(t3, m, half, True)
            d2[2 * m, half] = d2[2 * m, half] + first
            d2[2 * m + 1, half] = d2[2 * m + 1, half] + second

    loop(9, add_2, 3)
    clear_edges(d2, 3, 12)
    prolong_cols(d2, t2, 18, 16, False)

    def add_1(m):
        for half in range(2):
            first, second = prolong_rows(t2, m, half, False)
            d1[2 * m, half] = d1[2 * m, half] + first
            d1[2 * m + 1, half] = d1[2 * m + 1, half] + second

    loop(14, add_1, 2)
    clear_edges(d1, 2, 24)
    prolong_cols(d1, t1, 28, 24, False)

    def finish(m):
        for half in range(2):
            lanes = slice(half * LANE, (half + 1) * LANE)
            first, second = prolong_rows(t1, m, half, False)
            out[2 * m, :, lanes] = (d0[2 * m, half] + first) * sd[2 * m, half]
            out[2 * m + 1, :, lanes] = (d0[2 * m + 1, half] + second) * sd[2 * m + 1, half]

    loop(24, finish, 2)
    for make, gen in list(open_receives):
        arrive(make, gen)
    for make, gen in open_sends:
        sent(make, gen)


def solution(mesh):
    size_x, size_y = mesh.shape["gx"], mesh.shape["gy"]

    def body(field, stdev, mixing, gen_weight):
        def vmem(*shape, dtype=jnp.float32):
            return pltpu.VMEM(shape, dtype)

        def planes(x, y):
            return vmem(x, 2, y, LANE)

        return pl.pallas_call(
            functools.partial(kernel, size_x, size_y),
            out_shape=pltpu.VMEM(field.shape, jnp.float32),
            in_specs=[pl.BlockSpec(memory_space=pl.ANY)] * 4,
            out_specs=pl.BlockSpec(memory_space=pltpu.VMEM),
            scratch_shapes=[
                planes(54, 48), planes(34, 24), planes(24, 16), planes(18, 8),
                planes(48, 48), vmem(4, 256, 256), vmem(4, 256), vmem(4, 768, 256, dtype=jnp.bfloat16),
                planes(28, 72), planes(18, 56), planes(12, 40),
                planes(28, 32), planes(18, 24), planes(12, 16),
                vmem(2, 2, 2, 24, LANE), vmem(2, 3, 2, 16, LANE), vmem(2, 3, 2, 8, LANE),
                vmem(2, 24, 2, 8, LANE), vmem(2, 12, 2, 8, LANE), vmem(2, 6, 2, 8, LANE),
                vmem(4, 2, 2, 8, LANE), vmem(4, 3, 2, 8, LANE), vmem(4, 3, 2, 8, LANE),
                planes(48, 64), planes(28, 48), planes(18, 32), planes(12, 24),
                planes(48, 48), planes(28, 32), planes(18, 24), planes(12, 16),
                planes(48, 48), planes(28, 32), planes(18, 24), planes(12, 16),
                planes(28, 48), planes(18, 32), planes(12, 24),
                pltpu.SemaphoreType.DMA((18,)),
                pltpu.SemaphoreType.DMA((40,)),
                pltpu.SemaphoreType.DMA((40,)),
            ],
            compiler_params=pltpu.CompilerParams(
                collective_id=0, has_side_effects=True, vmem_limit_bytes=44 * 2**20
            ),
            cost_estimate=pl.CostEstimate(flops=2 * 3556 * 768 * 256, bytes_accessed=8 * 2**20, transcendentals=0),
            name="multigrid",
        )(*[pltpu.with_memory_space_constraint(a, pltpu.HBM) for a in (field, stdev, mixing, gen_weight)])

    return jax.shard_map(
        body,
        mesh=mesh,
        in_specs=(P("gx", "gy", None), P("gx", "gy", None), P(), P()),
        out_specs=P("gx", "gy", None),
        check_vma=False,
    )
```

```python
import functools

import jax
import jax.numpy as jnp
from jax import lax
from jax.experimental import pallas as pl
from jax.experimental.pallas import tpu as pltpu
from jax.sharding import PartitionSpec as P

RAD = 3
GENS = 4
LANE = 128
MESH = pl.DeviceIdType.MESH
DIRS = [(1, 0), (-1, 0), (0, 1), (0, -1), (1, 1), (1, -1), (-1, 1), (-1, -1)]
N = (48, 24, 12, 6)
RIM = (3, 5, 6, 6)
OUT = (0, 2, 3, 3)
YO = 8

_total = sum((1.0 - (k / (RAD + 1.0)) ** 2) ** 2 for k in range(-RAD, RAD + 1))
B = [(1.0 - (k / (RAD + 1.0)) ** 2) ** 2 / _total for k in range(RAD + 1)]
DOWN = [B[3], B[2] + B[3], B[1] + B[2], B[0] + B[1], B[0] + B[1], B[1] + B[2], B[2] + B[3], B[3]]
EVEN = [B[3], B[1] + B[2], B[0] + B[1], B[2] + B[3]]
ODD = EVEN[::-1]


def loop(count, step, unroll=1):
    def one(i, carry):
        step(i)
        return carry

    lax.fori_loop(0, count, one, 0, unroll=unroll)


def filtered(load):
    return load(3) * B[0] + (load(2) + load(4)) * B[1] + (load(1) + load(5)) * B[2] + (load(0) + load(6)) * B[3]


def restricted(load):
    return (
        (load(3) + load(4)) * DOWN[3]
        + (load(2) + load(5)) * DOWN[2]
        + (load(1) + load(6)) * DOWN[1]
        + (load(0) + load(7)) * DOWN[0]
    )


def dotted(weights, parts, scale=1.0):
    total = parts[0] * (weights[0] * scale)
    for weight, part in zip(weights[1:], parts[1:]):
        total = total + part * (weight * scale)
    return total


def restrict_rows(src, first, count, dst, span, shift, cols, dst_first, src_first=0):
    whole = [i for i in span if 2 * i - shift >= 0 and 2 * i - shift + 7 < count]
    low, high = whole[0], whole[-1] + 1
    src_cols, dst_cols = slice(src_first, src_first + cols), slice(dst_first, dst_first + cols)
    for half in range(2):
        for i in [i for i in span if i not in whole]:
            taps = [t for t in range(8) if 0 <= 2 * i - shift + t < count]
            parts = [src[first + 2 * i - shift + t, half, src_cols] for t in taps]
            dst[i, half, dst_cols] = dotted([DOWN[t] for t in taps], parts, 0.5)

    def step(j):
        for half in range(2):
            base = first + 2 * (j + low) - shift
            dst[j + low, half, dst_cols] = restricted(lambda t: src[base + t, half, src_cols]) * 0.5

    loop(high - low, step, 4)


def restrict_cols(src, start, dst, rows, cols):
    def step(i):
        for half in range(2):
            dst[i, half] = restricted(lambda t: src[i, half, pl.ds(start + t, cols, stride=2)])

    loop(rows, step, 2)


def filter_cols(src, start, dst, rows, cols, first=0):
    def step(j):
        i = first + j
        for half in range(2):
            dst[i, half] = filtered(lambda t: src[i, half, pl.ds(start + t, cols)])

    loop(rows, step, 2)


def filter_rows(src, dst, rows, first=0):
    def step(j):
        i = first + j
        for half in range(2):
            dst[i, half] = filtered(lambda t: src[i + t, half])

    loop(rows, step, 2)


def prolong_cols(src, dst, rows, count, odd_first, first=0):
    def step(j):
        i = first + j
        for half in range(2):
            parts = [src[i, half, pl.ds(t, count)] for t in range(4 if odd_first else 5)]
            if odd_first:
                lead, next_one = dotted(ODD, parts), dotted(EVEN, parts)
            else:
                lead, next_one = dotted(EVEN, parts[:4]), dotted(ODD, parts[1:])
            dst[i, half, pl.ds(0, count, stride=2)] = lead
            dst[i, half, pl.ds(1, count, stride=2)] = next_one

    loop(rows, step, 2)


def prolong_rows(src, m, half, odd_first):
    parts = [src[m + t, half] for t in range(4 if odd_first else 5)]
    if odd_first:
        return dotted(ODD, parts, 0.5), dotted(EVEN, parts, 0.5)
    return dotted(EVEN, parts[:4], 0.5), dotted(ODD, parts[1:], 0.5)


def mix(src, dst, weights, gen, first, rows_each, steps, cols):
    count = rows_each * cols

    def step(i):
        rows = pl.ds(first + i * rows_each, rows_each)
        cells = jnp.concatenate([src[rows, half].reshape(count, LANE) for half in range(2)], axis=1)
        high = cells.astype(jnp.bfloat16)
        low = (cells - high.astype(jnp.float32)).astype(jnp.bfloat16)
        product = jnp.dot(
            jnp.concatenate([high, high, low], axis=1), weights[gen], preferred_element_type=jnp.float32
        )
        for half in range(2):
            dst[rows, half] = product[:, half * LANE : (half + 1) * LANE].reshape(rows_each, cols, LANE)

    loop(steps, step)


def kernel(
    size_x, size_y, field, stdev, mixing, gen_weight, d0, d1, sd,
    f0, u0, u1, u2, u3, mats, gains, weights,
    x1, x2, x3, c1, c2, c3,
    rx1, rx2, rx3, ry1, ry2, ry3, rc1, rc2, rc3,
    y0, y1, y2, y3, k0, k1, k2, k3, d2, d3, t2, t3,
    load_sem, send_sem, recv_sem,
):
    gx, gy = lax.axis_index("gx"), lax.axis_index("gy")
    west, east = gx == 0, gx == size_x - 1
    south, north = gy == 0, gy == size_y - 1
    ext = (u0, u1, u2, u3)
    landings = ((rx1, ry1, rc1), (rx2, ry2, rc2), (rx3, ry3, rc3))

    def there(d):
        nx, ny = gx + d[0], gy + d[1]
        return (nx >= 0) & (nx < size_x) & (ny >= 0) & (ny < size_y)

    def against(d):
        return (-d[0], -d[1])

    loads = []
    for row, count in ((0, 24), (24, 24)):
        rows = pl.ds(row, count)
        for src, dst in ((field, f0), (stdev, sd)):
            loads.append(pltpu.make_async_copy(src.at[rows], dst.at[rows], load_sem.at[len(loads)]))
    for src, dst in ((mixing, mats), (gen_weight, gains)):
        loads.append(pltpu.make_async_copy(src, dst, load_sem.at[len(loads)]))
    for copy in loads[:4]:
        copy.start()

    barrier = pltpu.get_barrier_semaphore()
    for d in DIRS:

        @pl.when(there(d))
        def _():
            pl.semaphore_signal(barrier, inc=1, device_id=(gx + d[0], gy + d[1]), device_id_type=MESH)

    def remote(src, dst, slot, d):
        return pltpu.make_async_remote_copy(
            src_ref=src, dst_ref=dst, send_sem=send_sem.at[slot], recv_sem=recv_sem.at[slot],
            device_id=(gx + d[0], gy + d[1]), device_id_type=MESH,
        )

    def rim_span(step, first, n, rim):
        if step > 0:
            return pl.ds(first + n - rim, rim), pl.ds(first - rim, rim)
        return pl.ds(first, rim), pl.ds(first + n, rim)

    def gather_x(gen, k):
        n, rim, buf = N[gen], RIM[gen], ext[gen]
        src, dst = rim_span(DIRS[k][0], rim, n, rim)
        cols = pl.ds(YO, n)
        return remote(buf.at[src, :, cols], buf.at[dst, :, cols], gen * 2 + k, DIRS[k])

    def gather_y(gen, k):
        n, rim, buf = N[gen], RIM[gen], ext[gen]
        src, dst = rim_span(DIRS[k][1], YO, n, rim)
        rows = pl.ds(rim, n)
        return remote(buf.at[rows, :, src], buf.at[rows, :, dst], 8 + gen * 2 + k - 2, DIRS[k])

    def gather_corner(gen, k):
        n, rim, buf = N[gen], RIM[gen], ext[gen]
        src, dst = rim_span(DIRS[k % 4][1], YO, n, rim)
        rows = pl.ds(rim + n if k < 4 else 0, rim)
        return remote(buf.at[rows, :, src], buf.at[rows, :, dst], 48 + gen * 4 + k % 2 + k // 4 * 2, DIRS[k % 4])

    def gather_0(gen, k):
        d, n, rim = DIRS[k], N[0], RIM[0]
        (sx, tx), (sy, ty) = [
            (pl.ds(first, n), pl.ds(first, n)) if step == 0 else rim_span(step, first, n, rim)
            for step, first in ((d[0], rim), (d[1], YO))
        ]
        return remote(u0.at[sx, :, sy], u0.at[tx, :, ty], 40 + k, d)

    def scatter(gen, k):
        d, n, e, buf = DIRS[k], N[gen], OUT[gen], (c1, c2, c3)[gen - 1]
        rx, ry, rc = landings[gen - 1]
        if k < 2:
            dst = rx.at[k, :, :, pl.ds(0, n)]
        elif k < 4:
            dst = ry.at[k - 2, :, :, pl.ds(0, e)]
        else:
            dst = rc.at[k - 4, :, :, pl.ds(0, e)]

        def span(step):
            return pl.ds(e, n) if step == 0 else pl.ds(n + e, e) if step > 0 else pl.ds(0, e)

        return remote(buf.at[span(d[0]), :, span(d[1])], dst, 16 + (gen - 1) * 8 + k, d)

    ways = {
        gather_x: (0, 1),
        gather_y: (2, 3),
        gather_corner: (2, 3, 6, 7),
        gather_0: (0, 1, 4, 5, 6, 7),
        scatter: (0, 1, 2, 3, 4, 5, 6, 7),
    }
    open_sends, open_receives = [], []

    def goes(make, k):
        if make is gather_corner:
            return there(DIRS[k % 4]) & there(DIRS[k // 4])
        return there(DIRS[k])

    def comes(make, k):
        if make is gather_corner:
            return there(against(DIRS[k % 4])) & there(DIRS[k // 4])
        return there(against(DIRS[k]))

    def start(make, gen):
        open_sends.append((make, gen))
        open_receives.append((make, gen))
        for k in ways[make]:
            pl.when(goes(make, k))(lambda k=k: make(gen, k).start())

    def arrive(make, gen):
        open_receives.remove((make, gen))
        for k in ways[make]:
            pl.when(comes(make, k))(lambda k=k: make(gen, k).wait_recv())

    def sent(make, gen):
        for k in ways[make]:
            pl.when(goes(make, k))(lambda k=k: make(gen, k).wait_send())

    def clear_cols(buf, rows, first, count):
        def step(i):
            buf[i, :, first : first + count] = jnp.zeros((2, count, LANE), jnp.float32)

        loop(rows, step, 2)

    def clear_rows(buf, first, count):
        for i in range(count):
            buf[first + i] = jnp.zeros(buf.shape[1:], jnp.float32)

    def clear_edges(buf, width, n):
        pl.when(west)(lambda: clear_rows(buf, 0, width))
        pl.when(east)(lambda: clear_rows(buf, width + n, width))
        pl.when(south)(lambda: clear_cols(buf, n + 2 * width, 0, width))
        pl.when(north)(lambda: clear_cols(buf, n + 2 * width, width + n, width))

    clear_cols(x1, 28, 0, 8)
    clear_cols(x1, 28, 56, 16)
    clear_cols(x2, 18, 0, 8)
    clear_cols(x2, 18, 40, 16)
    clear_cols(x3, 12, 0, 8)
    clear_cols(x3, 12, 32, 8)
    for gen in range(GENS):
        n, rim, buf = N[gen], RIM[gen], ext[gen]
        pl.when(west)(lambda: clear_rows(buf, 0, rim))
        pl.when(east)(lambda: clear_rows(buf, rim + n, rim))
        pl.when(south)(lambda: clear_cols(buf, n + 2 * rim, YO - rim, rim))
        pl.when(north)(lambda: clear_cols(buf, n + 2 * rim, YO + n, rim))
    for gen in range(1, GENS):
        rx, ry, rc = landings[gen - 1]
        for k in range(8):
            buf, at = (rx, k) if k < 2 else (ry, k - 2) if k < 4 else (rc, k - 4)

            @pl.when(jnp.logical_not(there(against(DIRS[k]))))
            def _():
                buf[at] = jnp.zeros(buf.shape[1:], jnp.float32)

    def scale_rows(row, count):
        def step(i):
            for half in range(2):
                lanes = slice(half * LANE, (half + 1) * LANE)
                u0[RAD + row + i, half, YO : YO + N[0]] = f0[row + i, :, lanes] * sd[row + i, :, lanes]

        loop(count, step, 2)

    for copy in loads[:2]:
        copy.wait()
    scale_rows(0, 24)
    restrict_rows(u0, RAD, N[0], x1, range(0, 12), 7, N[0], YO, YO)
    for copy in loads[2:4]:
        copy.wait()
    for copy in loads[4:]:
        copy.start()
    scale_rows(24, 24)
    near_x = 3 - west.astype(jnp.int32) - east.astype(jnp.int32)
    near_y = 3 - south.astype(jnp.int32) - north.astype(jnp.int32)
    pl.semaphore_wait(barrier, near_x * near_y - 1)
    restrict_rows(u0, RAD, N[0], x1, range(12, 28), 7, N[0], YO, YO)
    restrict_cols(x1, 1, c1, 28, 32)
    clear_edges(c1, 2, 24)
    restrict_rows(c1, 0, 28, x2, range(18), 7, 32, 8)
    restrict_cols(x2, 1, c2, 18, 24)
    clear_edges(c2, 3, 12)
    start(scatter, 2)
    restrict_rows(c2, 0, 18, x3, range(12), 6, 24, 8)
    restrict_cols(x3, 2, c3, 12, 16)
    start(scatter, 3)
    start(scatter, 1)
    start(gather_y, 0)
    for copy in loads[4:]:
        copy.wait()
    for gen in range(GENS):

        def split(i, gen=gen):
            scaled = mats[gen, pl.ds(pl.multiple_of(i * 64, 64), 64), :] * gains[gen : gen + 1, :]
            high = scaled.astype(jnp.bfloat16)
            low = (scaled - high.astype(jnp.float32)).astype(jnp.bfloat16)
            for place, part in ((0, high), (256, low), (512, high)):
                weights[gen, pl.ds(pl.multiple_of(i * 64 + place, 64), 64), :] = part

        loop(4, split)
    def add_up(gen):
        n, e, rim, buf, own = N[gen], OUT[gen], RIM[gen], ext[gen], (c1, c2, c3)[gen - 1]
        rx, ry, rc = landings[gen - 1]
        inner, low, high = slice(YO, YO + n), slice(YO, YO + e), slice(YO + n - e, YO + n)

        def step(i):
            for half in range(2):
                buf[rim + i, half, inner] = own[e + i, half, e : e + n]
                buf[rim + i, half, low] = buf[rim + i, half, low] + ry[0, i, half, 0:e]
                buf[rim + i, half, high] = buf[rim + i, half, high] + ry[1, i, half, 0:e]

        loop(n, step, 2)
        for i in range(e):
            for half in range(2):
                for side, row in ((0, rim + i), (1, rim + n - e + i)):
                    buf[row, half, inner] = buf[row, half, inner] + rx[side, i, half, 0:n]
                    buf[row, half, low] = buf[row, half, low] + rc[2 * side, i, half, 0:e]
                    buf[row, half, high] = buf[row, half, high] + rc[2 * side + 1, i, half, 0:e]

    for gen in (3, 2, 1):
        arrive(scatter, gen)
        add_up(gen)
        start(gather_x, gen)
        start(gather_y, gen)
    arrive(gather_y, 0)
    filter_cols(u0, YO - RAD, y0, N[0], N[0], RAD)
    filter_rows(y0, k0, 42, RAD)
    mix(k0, d0, weights, 0, 3, 14, 1, N[0])
    for gen in (3, 2, 1):
        arrive(gather_x, gen)
        start(gather_corner, gen)
        if gen == 2:
            start(gather_0, 0)
    for gen in (3, 2, 1):
        arrive(gather_y, gen)
    filter_cols(u1, YO - 5, y1, 24, 32, 5)
    filter_rows(y1, k1, 18, 5)
    mix(k0, d0, weights, 0, 17, 14, 2, N[0])
    arrive(gather_corner, 3)
    filter_cols(u3, YO - 6, y3, 18, 16)
    filter_rows(y3, k3, 12)
    mix(k3, d3, weights, 3, 0, 12, 1, 16)
    clear_edges(d3, 3, 6)
    prolong_cols(d3, t3, 12, 12, True)
    arrive(gather_corner, 2)
    filter_cols(u2, YO - 6, y2, 24, 24)
    filter_rows(y2, k2, 18)
    mix(k2, d2, weights, 2, 0, 18, 1, 24)

    def add_2(m):
        for half in range(2):
            first, second = prolong_rows(t3, m, half, True)
            d2[2 * m, half] = d2[2 * m, half] + first
            d2[2 * m + 1, half] = d2[2 * m + 1, half] + second

    loop(9, add_2, 3)
    clear_edges(d2, 3, 12)
    prolong_cols(d2, t2, 18, 16, False)
    arrive(gather_corner, 1)
    for first in (0, 29):
        filter_cols(u1, YO - 5, y1, 5, 32, first)
    for first in (0, 23):
        filter_rows(y1, k1, 5, first)
    mix(k1, d1, weights, 1, 0, 14, 2, 32)

    def add_1(m):
        for half in range(2):
            first, second = prolong_rows(t2, m, half, False)
            d1[2 * m, half] = d1[2 * m, half] + first
            d1[2 * m + 1, half] = d1[2 * m + 1, half] + second

    loop(14, add_1, 2)
    clear_edges(d1, 2, 24)
    arrive(gather_0, 0)
    filter_cols(u0, YO - RAD, y0, RAD, N[0])
    filter_cols(u0, YO - RAD, y0, RAD, N[0], N[0] + RAD)
    for first in (0, N[0] - RAD):
        filter_rows(y0, k0, RAD, first)
        mix(k0, d0, weights, 0, first, RAD, 1, N[0])
    for make, gen in list(open_receives):
        arrive(make, gen)
    for make, gen in open_sends:
        sent(make, gen)


def finish(d0, d1, sd, out, t1, rows, sems):
    copies = []
    for part in range(6):
        first = 0 if part == 0 else 4 * part + 4
        prolong_cols(d1, t1, 4 * part + 8 - first, 24, False, first)

        def step(j, part=part):
            m = 4 * part + j
            for half in range(2):
                lanes = slice(half * LANE, (half + 1) * LANE)
                even, odd = prolong_rows(t1, m, half, False)
                rows[2 * m, :, lanes] = (d0[2 * m, half] + even) * sd[2 * m, :, lanes]
                rows[2 * m + 1, :, lanes] = (d0[2 * m + 1, half] + odd) * sd[2 * m + 1, :, lanes]

        loop(4, step, 2)
        some = pl.ds(8 * part, 8)
        copies.append(pltpu.make_async_copy(rows.at[some], out.at[some], sems.at[part]))
        copies[-1].start()
    for copy in copies:
        copy.wait()


def solution(mesh):
    size_x, size_y = mesh.shape["gx"], mesh.shape["gy"]

    def body(field, stdev, mixing, gen_weight):
        def vmem(*shape, dtype=jnp.float32):
            return pltpu.VMEM(shape, dtype)

        def planes(x, y):
            return vmem(x, 2, y, LANE)

        inputs = [pltpu.with_memory_space_constraint(a, pltpu.HBM) for a in (field, stdev, mixing, gen_weight)]
        held = pl.BlockSpec(memory_space=pltpu.VMEM)
        parts = pl.pallas_call(
            functools.partial(kernel, size_x, size_y),
            out_shape=(planes(48, 48), planes(28, 32), vmem(*field.shape)),
            in_specs=[pl.BlockSpec(memory_space=pl.ANY)] * 4,
            out_specs=(held, held, held),
            scratch_shapes=[
                vmem(*field.shape), planes(54, 64), planes(34, 48), planes(24, 32), planes(18, 24),
                vmem(4, 256, 256), vmem(4, 256), vmem(4, 768, 256, dtype=jnp.bfloat16),
                planes(28, 72), planes(18, 56), planes(12, 40),
                planes(28, 32), planes(18, 24), planes(12, 16),
                vmem(2, 2, 2, 24, LANE), vmem(2, 3, 2, 16, LANE), vmem(2, 3, 2, 8, LANE),
                vmem(2, 24, 2, 8, LANE), vmem(2, 12, 2, 8, LANE), vmem(2, 6, 2, 8, LANE),
                vmem(4, 2, 2, 8, LANE), vmem(4, 3, 2, 8, LANE), vmem(4, 3, 2, 8, LANE),
                planes(54, 48), planes(34, 32), planes(24, 24), planes(18, 16),
                planes(48, 48), planes(28, 32), planes(18, 24), planes(12, 16),
                planes(18, 24), planes(12, 16),
                planes(18, 32), planes(12, 24),
                pltpu.SemaphoreType.DMA((6,)),
                pltpu.SemaphoreType.DMA((64,)),
                pltpu.SemaphoreType.DMA((64,)),
            ],
            compiler_params=pltpu.CompilerParams(
                collective_id=0, has_side_effects=True, vmem_limit_bytes=40 * 2**20
            ),
            cost_estimate=pl.CostEstimate(flops=2 * 3556 * 768 * 256, bytes_accessed=8 * 2**20, transcendentals=0),
            name="multigrid",
        )(*inputs)
        return pl.pallas_call(
            finish,
            out_shape=jax.ShapeDtypeStruct(field.shape, jnp.float32),
            in_specs=[held] * 3,
            out_specs=pl.BlockSpec(memory_space=pl.ANY),
            scratch_shapes=[planes(28, 48), vmem(*field.shape), pltpu.SemaphoreType.DMA((6,))],
            compiler_params=pltpu.CompilerParams(vmem_limit_bytes=12 * 2**20),
            name="finish",
        )(*[pltpu.with_memory_space_constraint(a, pltpu.VMEM) for a in parts])

    return jax.shard_map(
        body,
        mesh=mesh,
        in_specs=(P("gx", "gy", None), P("gx", "gy", None), P(), P()),
        out_specs=P("gx", "gy", None),
        check_vma=False,
    )
```

```python
import functools

import jax
import jax.numpy as jnp
from jax import lax
from jax.experimental import pallas as pl
from jax.experimental.pallas import tpu as pltpu
from jax.sharding import PartitionSpec as P

RAD = 3
GENS = 4
LANE = 128
MESH = pl.DeviceIdType.MESH
DIRS = [(1, 0), (-1, 0), (0, 1), (0, -1), (1, 1), (1, -1), (-1, 1), (-1, -1)]
N = (48, 24, 12, 6)
RIM = (3, 5, 6, 6)
OUT = (0, 2, 3, 3)
YO = 8

_total = sum((1.0 - (k / (RAD + 1.0)) ** 2) ** 2 for k in range(-RAD, RAD + 1))
B = [(1.0 - (k / (RAD + 1.0)) ** 2) ** 2 / _total for k in range(RAD + 1)]
DOWN = [B[3], B[2] + B[3], B[1] + B[2], B[0] + B[1], B[0] + B[1], B[1] + B[2], B[2] + B[3], B[3]]
EVEN = [B[3], B[1] + B[2], B[0] + B[1], B[2] + B[3]]
ODD = EVEN[::-1]


def loop(count, step, unroll=1):
    def one(i, carry):
        step(i)
        return carry

    lax.fori_loop(0, count, one, 0, unroll=unroll)


def filtered(load):
    return load(3) * B[0] + (load(2) + load(4)) * B[1] + (load(1) + load(5)) * B[2] + (load(0) + load(6)) * B[3]


def restricted(load):
    return (
        (load(3) + load(4)) * DOWN[3]
        + (load(2) + load(5)) * DOWN[2]
        + (load(1) + load(6)) * DOWN[1]
        + (load(0) + load(7)) * DOWN[0]
    )


def dotted(weights, parts, scale=1.0):
    total = parts[0] * (weights[0] * scale)
    for weight, part in zip(weights[1:], parts[1:]):
        total = total + part * (weight * scale)
    return total


def restrict_rows(src, first, count, dst, span, shift, cols, dst_first, src_first=0):
    whole = [i for i in span if 2 * i - shift >= 0 and 2 * i - shift + 7 < count]
    low, high = whole[0], whole[-1] + 1
    src_cols, dst_cols = slice(src_first, src_first + cols), slice(dst_first, dst_first + cols)
    for half in range(2):
        for i in [i for i in span if i not in whole]:
            taps = [t for t in range(8) if 0 <= 2 * i - shift + t < count]
            parts = [src[first + 2 * i - shift + t, half, src_cols] for t in taps]
            dst[i, half, dst_cols] = dotted([DOWN[t] for t in taps], parts, 0.5)

    def step(j):
        for half in range(2):
            base = first + 2 * (j + low) - shift
            dst[j + low, half, dst_cols] = restricted(lambda t: src[base + t, half, src_cols]) * 0.5

    loop(high - low, step, 4)


def restrict_cols(src, start, dst, rows, cols):
    def step(i):
        for half in range(2):
            dst[i, half] = restricted(lambda t: src[i, half, pl.ds(start + t, cols, stride=2)])

    loop(rows, step, 2)


def filter_cols(src, start, dst, rows, cols, first=0):
    def step(j):
        i = first + j
        for half in range(2):
            dst[i, half] = filtered(lambda t: src[i, half, pl.ds(start + t, cols)])

    loop(rows, step, 2)


def filter_rows(src, dst, rows, first=0):
    def step(j):
        i = first + j
        for half in range(2):
            dst[i, half] = filtered(lambda t: src[i + t, half])

    loop(rows, step, 2)


def prolong_cols(src, dst, rows, count, odd_first, first=0):
    def step(j):
        i = first + j
        for half in range(2):
            parts = [src[i, half, pl.ds(t, count)] for t in range(4 if odd_first else 5)]
            if odd_first:
                lead, next_one = dotted(ODD, parts), dotted(EVEN, parts)
            else:
                lead, next_one = dotted(EVEN, parts[:4]), dotted(ODD, parts[1:])
            dst[i, half, pl.ds(0, count, stride=2)] = lead
            dst[i, half, pl.ds(1, count, stride=2)] = next_one

    loop(rows, step, 2)


def prolong_rows(src, m, half, odd_first):
    parts = [src[m + t, half] for t in range(4 if odd_first else 5)]
    if odd_first:
        return dotted(ODD, parts, 0.5), dotted(EVEN, parts, 0.5)
    return dotted(EVEN, parts[:4], 0.5), dotted(ODD, parts[1:], 0.5)


def mix(src, dst, weights, gen, first, rows_each, steps, cols):
    count = rows_each * cols

    def step(i):
        rows = pl.ds(first + i * rows_each, rows_each)
        cells = jnp.concatenate([src[rows, half].reshape(count, LANE) for half in range(2)], axis=1)
        high = cells.astype(jnp.bfloat16)
        low = (cells - high.astype(jnp.float32)).astype(jnp.bfloat16)
        product = jnp.dot(
            jnp.concatenate([high, high, low], axis=1), weights[gen], preferred_element_type=jnp.float32
        )
        for half in range(2):
            dst[rows, half] = product[:, half * LANE : (half + 1) * LANE].reshape(rows_each, cols, LANE)

    loop(steps, step)


def kernel(
    size_x, size_y, field, stdev, mixing, gen_weight, d0, d1, sd,
    f0, u0, u1, u2, u3, mats, gains, weights,
    x1, x2, x3, c1, c2, c3,
    rx1, rx2, rx3, ry1, ry2, ry3, rc1, rc2, rc3,
    y0, y1, y2, y3, k0, k1, k2, k3, d2, d3, t2, t3,
    load_sem, send_sem, recv_sem,
):
    gx, gy = lax.axis_index("gx"), lax.axis_index("gy")
    west, east = gx == 0, gx == size_x - 1
    south, north = gy == 0, gy == size_y - 1
    ext = (u0, u1, u2, u3)
    landings = ((rx1, ry1, rc1), (rx2, ry2, rc2), (rx3, ry3, rc3))

    def there(d):
        nx, ny = gx + d[0], gy + d[1]
        return (nx >= 0) & (nx < size_x) & (ny >= 0) & (ny < size_y)

    def against(d):
        return (-d[0], -d[1])

    loads = []
    for row, count in ((0, 24), (24, 24)):
        rows = pl.ds(row, count)
        for src, dst in ((field, f0), (stdev, sd)):
            loads.append(pltpu.make_async_copy(src.at[rows], dst.at[rows], load_sem.at[len(loads)]))
    for src, dst in ((mixing, mats), (gen_weight, gains)):
        loads.append(pltpu.make_async_copy(src, dst, load_sem.at[len(loads)]))
    for copy in loads[:4]:
        copy.start()

    barrier = pltpu.get_barrier_semaphore()
    for d in DIRS:

        @pl.when(there(d))
        def _():
            pl.semaphore_signal(barrier, inc=1, device_id=(gx + d[0], gy + d[1]), device_id_type=MESH)

    def remote(src, dst, slot, d):
        return pltpu.make_async_remote_copy(
            src_ref=src, dst_ref=dst, send_sem=send_sem.at[slot], recv_sem=recv_sem.at[slot],
            device_id=(gx + d[0], gy + d[1]), device_id_type=MESH,
        )

    def rim_span(step, first, n, rim):
        if step > 0:
            return pl.ds(first + n - rim, rim), pl.ds(first - rim, rim)
        return pl.ds(first, rim), pl.ds(first + n, rim)

    def gather_x(gen, k):
        n, rim, buf = N[gen], RIM[gen], ext[gen]
        src, dst = rim_span(DIRS[k][0], rim, n, rim)
        cols = pl.ds(YO, n)
        return remote(buf.at[src, :, cols], buf.at[dst, :, cols], gen * 2 + k, DIRS[k])

    def gather_y(gen, k):
        n, rim, buf = N[gen], RIM[gen], ext[gen]
        src, dst = rim_span(DIRS[k][1], YO, n, rim)
        rows = pl.ds(rim, n)
        return remote(buf.at[rows, :, src], buf.at[rows, :, dst], 8 + gen * 2 + k - 2, DIRS[k])

    def gather_corner(gen, k):
        n, rim, buf = N[gen], RIM[gen], ext[gen]
        src, dst = rim_span(DIRS[k % 4][1], YO, n, rim)
        rows = pl.ds(rim + n if k < 4 else 0, rim)
        return remote(buf.at[rows, :, src], buf.at[rows, :, dst], 48 + gen * 4 + k % 2 + k // 4 * 2, DIRS[k % 4])

    def gather_0(gen, k):
        d, n, rim = DIRS[k], N[0], RIM[0]
        (sx, tx), (sy, ty) = [
            (pl.ds(first, n), pl.ds(first, n)) if step == 0 else rim_span(step, first, n, rim)
            for step, first in ((d[0], rim), (d[1], YO))
        ]
        return remote(u0.at[sx, :, sy], u0.at[tx, :, ty], 40 + k, d)

    def scatter(gen, k):
        d, n, e, buf = DIRS[k], N[gen], OUT[gen], (c1, c2, c3)[gen - 1]
        rx, ry, rc = landings[gen - 1]
        if k < 2:
            dst = rx.at[k, :, :, pl.ds(0, n)]
        elif k < 4:
            dst = ry.at[k - 2, :, :, pl.ds(0, e)]
        else:
            dst = rc.at[k - 4, :, :, pl.ds(0, e)]

        def span(step):
            return pl.ds(e, n) if step == 0 else pl.ds(n + e, e) if step > 0 else pl.ds(0, e)

        return remote(buf.at[span(d[0]), :, span(d[1])], dst, 16 + (gen - 1) * 8 + k, d)

    ways = {
        gather_x: (0, 1),
        gather_y: (2, 3),
        gather_corner: (2, 3, 6, 7),
        gather_0: (4, 5, 6, 7, 0, 1),
        scatter: (4, 5, 6, 7, 0, 1, 2, 3),
    }
    open_sends, open_receives = [], []

    def goes(make, k):
        if make is gather_corner:
            return there(DIRS[k % 4]) & there(DIRS[k // 4])
        return there(DIRS[k])

    def comes(make, k):
        if make is gather_corner:
            return there(against(DIRS[k % 4])) & there(DIRS[k // 4])
        return there(against(DIRS[k]))

    def start(make, gen):
        open_sends.append((make, gen))
        open_receives.append((make, gen))
        for k in ways[make]:
            pl.when(goes(make, k))(lambda k=k: make(gen, k).start())

    def arrive(make, gen):
        open_receives.remove((make, gen))
        for k in ways[make]:
            pl.when(comes(make, k))(lambda k=k: make(gen, k).wait_recv())

    def sent(make, gen):
        for k in ways[make]:
            pl.when(goes(make, k))(lambda k=k: make(gen, k).wait_send())

    def clear_cols(buf, rows, first, count):
        def step(i):
            buf[i, :, first : first + count] = jnp.zeros((2, count, LANE), jnp.float32)

        loop(rows, step, 2)

    def clear_rows(buf, first, count):
        for i in range(count):
            buf[first + i] = jnp.zeros(buf.shape[1:], jnp.float32)

    def clear_edges(buf, width, n):
        pl.when(west)(lambda: clear_rows(buf, 0, width))
        pl.when(east)(lambda: clear_rows(buf, width + n, width))
        pl.when(south)(lambda: clear_cols(buf, n + 2 * width, 0, width))
        pl.when(north)(lambda: clear_cols(buf, n + 2 * width, width + n, width))

    clear_cols(x1, 28, 0, 8)
    clear_cols(x1, 28, 56, 16)
    clear_cols(x2, 18, 0, 8)
    clear_cols(x2, 18, 40, 16)
    clear_cols(x3, 12, 0, 8)
    clear_cols(x3, 12, 32, 8)
    for gen in range(GENS):
        n, rim, buf = N[gen], RIM[gen], ext[gen]
        pl.when(west)(lambda: clear_rows(buf, 0, rim))
        pl.when(east)(lambda: clear_rows(buf, rim + n, rim))
        pl.when(south)(lambda: clear_cols(buf, n + 2 * rim, YO - rim, rim))
        pl.when(north)(lambda: clear_cols(buf, n + 2 * rim, YO + n, rim))
    for gen in range(1, GENS):
        rx, ry, rc = landings[gen - 1]
        for k in range(8):
            buf, at = (rx, k) if k < 2 else (ry, k - 2) if k < 4 else (rc, k - 4)

            @pl.when(jnp.logical_not(there(against(DIRS[k]))))
            def _():
                buf[at] = jnp.zeros(buf.shape[1:], jnp.float32)

    def scale_rows(row, count):
        def step(i):
            for half in range(2):
                lanes = slice(half * LANE, (half + 1) * LANE)
                u0[RAD + row + i, half, YO : YO + N[0]] = f0[row + i, :, lanes] * sd[row + i, :, lanes]

        loop(count, step, 2)

    for copy in loads[:2]:
        copy.wait()
    scale_rows(0, 24)
    restrict_rows(u0, RAD, N[0], x1, range(0, 12), 7, N[0], YO, YO)
    for copy in loads[2:4]:
        copy.wait()
    for copy in loads[4:]:
        copy.start()
    scale_rows(24, 24)
    near_x = 3 - west.astype(jnp.int32) - east.astype(jnp.int32)
    near_y = 3 - south.astype(jnp.int32) - north.astype(jnp.int32)
    pl.semaphore_wait(barrier, near_x * near_y - 1)
    restrict_rows(u0, RAD, N[0], x1, range(12, 28), 7, N[0], YO, YO)
    restrict_cols(x1, 1, c1, 28, 32)
    clear_edges(c1, 2, 24)
    restrict_rows(c1, 0, 28, x2, range(18), 7, 32, 8)
    restrict_cols(x2, 1, c2, 18, 24)
    clear_edges(c2, 3, 12)
    start(scatter, 2)
    restrict_rows(c2, 0, 18, x3, range(12), 6, 24, 8)
    restrict_cols(x3, 2, c3, 12, 16)
    start(scatter, 3)
    start(scatter, 1)
    start(gather_y, 0)
    for copy in loads[4:]:
        copy.wait()
    for gen in range(GENS):

        def split(i, gen=gen):
            scaled = mats[gen, pl.ds(pl.multiple_of(i * 64, 64), 64), :] * gains[gen : gen + 1, :]
            high = scaled.astype(jnp.bfloat16)
            low = (scaled - high.astype(jnp.float32)).astype(jnp.bfloat16)
            for place, part in ((0, high), (256, low), (512, high)):
                weights[gen, pl.ds(pl.multiple_of(i * 64 + place, 64), 64), :] = part

        loop(4, split)
    def add_up(gen):
        n, e, rim, buf, own = N[gen], OUT[gen], RIM[gen], ext[gen], (c1, c2, c3)[gen - 1]
        rx, ry, rc = landings[gen - 1]
        inner, low, high = slice(YO, YO + n), slice(YO, YO + e), slice(YO + n - e, YO + n)

        def step(i):
            for half in range(2):
                buf[rim + i, half, inner] = own[e + i, half, e : e + n]
                buf[rim + i, half, low] = buf[rim + i, half, low] + ry[0, i, half, 0:e]
                buf[rim + i, half, high] = buf[rim + i, half, high] + ry[1, i, half, 0:e]

        loop(n, step, 2)
        for i in range(e):
            for half in range(2):
                for side, row in ((0, rim + i), (1, rim + n - e + i)):
                    buf[row, half, inner] = buf[row, half, inner] + rx[side, i, half, 0:n]
                    buf[row, half, low] = buf[row, half, low] + rc[2 * side, i, half, 0:e]
                    buf[row, half, high] = buf[row, half, high] + rc[2 * side + 1, i, half, 0:e]

    for gen in (3, 2, 1):
        arrive(scatter, gen)
        add_up(gen)
        start(gather_x, gen)
        start(gather_y, gen)
    arrive(gather_y, 0)
    filter_cols(u0, YO - RAD, y0, N[0], N[0], RAD)
    filter_rows(y0, k0, 42, RAD)
    mix(k0, d0, weights, 0, 3, 14, 1, N[0])
    for gen in (3, 2, 1):
        arrive(gather_x, gen)
        start(gather_corner, gen)
        if gen == 2:
            start(gather_0, 0)
    for gen in (3, 2, 1):
        arrive(gather_y, gen)
    filter_cols(u1, YO - 5, y1, 24, 32, 5)
    filter_rows(y1, k1, 18, 5)
    mix(k0, d0, weights, 0, 17, 14, 2, N[0])
    arrive(gather_corner, 3)
    filter_cols(u3, YO - 6, y3, 18, 16)
    filter_rows(y3, k3, 12)
    mix(k3, d3, weights, 3, 0, 12, 1, 16)
    clear_edges(d3, 3, 6)
    prolong_cols(d3, t3, 12, 12, True)
    arrive(gather_corner, 2)
    filter_cols(u2, YO - 6, y2, 24, 24)
    filter_rows(y2, k2, 18)
    mix(k2, d2, weights, 2, 0, 18, 1, 24)

    def add_2(m):
        for half in range(2):
            first, second = prolong_rows(t3, m, half, True)
            d2[2 * m, half] = d2[2 * m, half] + first
            d2[2 * m + 1, half] = d2[2 * m + 1, half] + second

    loop(9, add_2, 3)
    clear_edges(d2, 3, 12)
    prolong_cols(d2, t2, 18, 16, False)
    arrive(gather_corner, 1)
    for first in (0, 29):
        filter_cols(u1, YO - 5, y1, 5, 32, first)
    for first in (0, 23):
        filter_rows(y1, k1, 5, first)
    mix(k1, d1, weights, 1, 0, 14, 2, 32)

    def add_1(m):
        for half in range(2):
            first, second = prolong_rows(t2, m, half, False)
            d1[2 * m, half] = d1[2 * m, half] + first
            d1[2 * m + 1, half] = d1[2 * m + 1, half] + second

    loop(14, add_1, 2)
    clear_edges(d1, 2, 24)
    arrive(gather_0, 0)
    filter_cols(u0, YO - RAD, y0, RAD, N[0])
    filter_cols(u0, YO - RAD, y0, RAD, N[0], N[0] + RAD)
    for first in (0, N[0] - RAD):
        filter_rows(y0, k0, RAD, first)
        mix(k0, d0, weights, 0, first, RAD, 1, N[0])
    for make, gen in list(open_receives):
        arrive(make, gen)
    for make, gen in open_sends:
        sent(make, gen)


def finish(d0, d1, sd, out, t1, rows, sems):
    copies = []
    for part in range(12):
        first = 0 if part == 0 else 2 * part + 4
        prolong_cols(d1, t1, 2 * part + 6 - first, 24, False, first)

        def step(j, part=part):
            m = 2 * part + j
            for half in range(2):
                lanes = slice(half * LANE, (half + 1) * LANE)
                even, odd = prolong_rows(t1, m, half, False)
                rows[2 * m, :, lanes] = (d0[2 * m, half] + even) * sd[2 * m, :, lanes]
                rows[2 * m + 1, :, lanes] = (d0[2 * m + 1, half] + odd) * sd[2 * m + 1, :, lanes]

        loop(2, step, 2)
        some = pl.ds(4 * part, 4)
        copies.append(pltpu.make_async_copy(rows.at[some], out.at[some], sems.at[part]))
        copies[-1].start()
    for copy in copies:
        copy.wait()


def solution(mesh):
    size_x, size_y = mesh.shape["gx"], mesh.shape["gy"]

    def body(field, stdev, mixing, gen_weight):
        def vmem(*shape, dtype=jnp.float32):
            return pltpu.VMEM(shape, dtype)

        def planes(x, y):
            return vmem(x, 2, y, LANE)

        inputs = [pltpu.with_memory_space_constraint(a, pltpu.HBM) for a in (field, stdev, mixing, gen_weight)]
        held = pl.BlockSpec(memory_space=pltpu.VMEM)
        parts = pl.pallas_call(
            functools.partial(kernel, size_x, size_y),
            out_shape=(planes(48, 48), planes(28, 32), vmem(*field.shape)),
            in_specs=[pl.BlockSpec(memory_space=pl.ANY)] * 4,
            out_specs=(held, held, held),
            scratch_shapes=[
                vmem(*field.shape), planes(54, 64), planes(34, 48), planes(24, 32), planes(18, 24),
                vmem(4, 256, 256), vmem(4, 256), vmem(4, 768, 256, dtype=jnp.bfloat16),
                planes(28, 72), planes(18, 56), planes(12, 40),
                planes(28, 32), planes(18, 24), planes(12, 16),
                vmem(2, 2, 2, 24, LANE), vmem(2, 3, 2, 16, LANE), vmem(2, 3, 2, 8, LANE),
                vmem(2, 24, 2, 8, LANE), vmem(2, 12, 2, 8, LANE), vmem(2, 6, 2, 8, LANE),
                vmem(4, 2, 2, 8, LANE), vmem(4, 3, 2, 8, LANE), vmem(4, 3, 2, 8, LANE),
                planes(54, 48), planes(34, 32), planes(24, 24), planes(18, 16),
                planes(48, 48), planes(28, 32), planes(18, 24), planes(12, 16),
                planes(18, 24), planes(12, 16),
                planes(18, 32), planes(12, 24),
                pltpu.SemaphoreType.DMA((6,)),
                pltpu.SemaphoreType.DMA((64,)),
                pltpu.SemaphoreType.DMA((64,)),
            ],
            compiler_params=pltpu.CompilerParams(
                collective_id=0, has_side_effects=True, vmem_limit_bytes=40 * 2**20
            ),
            cost_estimate=pl.CostEstimate(flops=2 * 3556 * 768 * 256, bytes_accessed=8 * 2**20, transcendentals=0),
            name="multigrid",
        )(*inputs)
        return pl.pallas_call(
            finish,
            out_shape=jax.ShapeDtypeStruct(field.shape, jnp.float32),
            in_specs=[held] * 3,
            out_specs=pl.BlockSpec(memory_space=pl.ANY),
            scratch_shapes=[planes(28, 48), vmem(*field.shape), pltpu.SemaphoreType.DMA((12,))],
            compiler_params=pltpu.CompilerParams(vmem_limit_bytes=12 * 2**20),
            name="finish",
        )(*[pltpu.with_memory_space_constraint(a, pltpu.VMEM) for a in parts])

    return jax.shard_map(
        body,
        mesh=mesh,
        in_specs=(P("gx", "gy", None), P("gx", "gy", None), P(), P()),
        out_specs=P("gx", "gy", None),
        check_vma=False,
    )
```
